32 devices in a mesh: group: 2 (over y), row: 8 (over z, core), chan: 2 (over x).
Axes of the slice: x: 2, y: 2, z: 4, core: 2. Of those that a mesh axis runs over, the one named last changes fastest.
Arguments:
- pair: bfloat16 [1024, 512, 128], P(('group', 'row'), 'chan'), parts along dimension 0, may hold values from -6 to 6
- token_mask: int32 [1024], P('group'), parts along dimension 0, may hold values 0 or 1
- band_start: int32 [2], P('group'), parts along dimension 0, may hold values from 0 to 496
- w_left: bfloat16 [128, 64], replicated, may hold values from -0.5 to 0.5
- w_left_gate: bfloat16 [128, 64], replicated, may hold values from -0.5 to 0.5
- w_right: bfloat16 [128, 64], replicated, may hold values from -0.5 to 0.5
- w_right_gate: bfloat16 [128, 64], replicated, may hold values from -0.5 to 0.5
- w_gate_out: bfloat16 [128, 128], replicated, may hold values from -0.5 to 0.5
- w_out: bfloat16 [64, 128], replicated, may hold values from -0.75 to 0.75
- norm_in_gain: float32 [128], replicated, may hold values from 0.1 to 1.9
- norm_out_gain: float32 [64], replicated, may hold values from 0.1 to 1.9
Outputs:
- band_update: bfloat16 [32, 512, 128], P(('group', 'row'), 'chan'), parts along dimension 0
The draws below stay inside these ranges and needn't reach their ends.
There are 2 independent parts, one for each index of `group`. The reference program is written for one: setup_inputs(seed, part) draws one part's arguments, and reference() takes and returns one part's arrays. A program takes and returns all parts, laid end to end along the dimension named above; an argument that names none is the same for every part. Nothing has to cross between parts.
Inputs may be any that keep to these rules, and one draw needn't show every extreme that they name: `band_start`: the band of 16 rows lies inside the map.
All inputs are finite; a program needn't handle non-finite values.
Results may differ from the reference program's by a relative error of at most 0.0087.
Values may be sent and summed in bfloat16 or wider, within the bound.
A program may use at most 128 MiB of HBM per device.

```python
import jax
import jax.numpy as jnp
from jax import lax

C = 128
CH = 64
ROWS_DEV = 64
TOKENS = 512
BAND = 16


def touch_ends(drawn, stream_key, smallest, top_value):
    place = [jax.random.randint(jax.random.fold_in(stream_key, axis), (), 0, length) for axis, length in enumerate(drawn.shape)]
    main_axis = drawn.shape.index(max(drawn.shape))
    neighbour = place[:main_axis] + [(place[main_axis] + 1) % drawn.shape[main_axis]] + place[main_axis + 1:]
    return drawn.at[tuple(place)].set(smallest).at[tuple(neighbour)].set(top_value)


def levels(rng, extent, shards, smallest, top_value):
    def one(position, blocks):
        heights = jax.random.uniform(jax.random.fold_in(jax.random.fold_in(rng, 6), position), (blocks,), jnp.float32, smallest / len(shards), top_value / len(shards))
        return jnp.repeat(jnp.exp(heights), extent[position] // blocks).reshape((-1,) + (1,) * (len(extent) - position - 1))

    level = one(*shards[0])
    for cut in shards[1:]:
        level = level * one(*cut)
    return level


def centred(own_key, dims, width, reach, cuts=(), kind=jnp.bfloat16):
    entries = jax.random.normal(own_key, dims, jnp.float32) * width
    if len(cuts) > 0:
        entries = levels(own_key, dims, cuts, -0.22, 0.18) * entries
    return jnp.clip(entries, min=-reach, max=reach).astype(kind)


def setup_inputs(seed: int = 0, part: int = 0) -> dict:
    streams_of = jax.random.split(jax.random.key(seed), 12)
    own_keys = jax.random.split(jax.random.fold_in(streams_of[11], part), 12)
    return {
        "pair": centred(own_keys[0], (TOKENS, TOKENS, C), 1.0, 6.0, ((0, 8), (1, 2))),
        "token_mask": touch_ends((jax.random.randint(own_keys[1], (TOKENS,), 0, 8) < 7).astype(jnp.int32), jax.random.fold_in(own_keys[1], 1), 0, 1),
        "band_start": jax.random.randint(own_keys[2], (1,), 0, TOKENS - BAND + 1).astype(jnp.int32),
        "w_left": centred(streams_of[3], (C, CH), C ** -0.5, 0.5),
        "w_left_gate": centred(streams_of[4], (C, CH), C ** -0.5, 0.5),
        "w_right": centred(streams_of[5], (C, CH), C ** -0.5, 0.5),
        "w_right_gate": centred(streams_of[6], (C, CH), C ** -0.5, 0.5),
        "w_gate_out": centred(streams_of[7], (C, C), C ** -0.5, 0.5),
        "w_out": centred(streams_of[8], (CH, C), CH ** -0.5, 0.75),
        "norm_in_gain": jnp.clip(1.0 + 0.18 * jax.random.normal(streams_of[9], (C,), jnp.float32), 0.1, 1.9),
        "norm_out_gain": jnp.clip(1.0 + 0.18 * jax.random.normal(streams_of[10], (CH,), jnp.float32), 0.1, 1.9),
    }


def layer_norm(values, gain):
    values = values.astype(jnp.float32)
    middle = lax.optimization_barrier(jnp.mean(values, -1, keepdims=True))
    spread = lax.optimization_barrier(jnp.mean(jnp.square(values - middle), -1, keepdims=True))
    return (values - middle) * lax.rsqrt(spread + 1e-05) * gain.astype(jnp.float32)

def gated(normed, w_value, w_gate):
    value = jnp.dot(normed, w_value, preferred_element_type=jnp.float32)
    opener = jnp.dot(normed, w_gate, preferred_element_type=jnp.float32)
    return jax.nn.sigmoid(opener) * value

def reference(pair, token_mask, band_start, w_left, w_left_gate, w_right, w_right_gate, w_gate_out, w_out, norm_in_gain, norm_out_gain):
    valid = token_mask.astype(jnp.float32)
    start = band_start[0].astype(jnp.int32)
    blocks = pair.reshape(TOKENS // ROWS_DEV, ROWS_DEV, TOKENS, C)
    mask_blocks = valid.reshape(TOKENS // ROWS_DEV, ROWS_DEV)

    def right_block(inputs):
        block, rows_valid = inputs
        normed = layer_norm(block, norm_in_gain).astype(jnp.bfloat16)
        factor = gated(normed, w_right, w_right_gate) * rows_valid[:, None, None] * valid[None, :, None]
        return factor.astype(jnp.bfloat16)
    right = lax.map(right_block, (blocks, mask_blocks))
    band = lax.dynamic_slice_in_dim(pair, start, BAND, 0)
    band_valid = lax.dynamic_slice_in_dim(valid, start, BAND, 0)
    normed = layer_norm(band, norm_in_gain).astype(jnp.bfloat16)
    left = (gated(normed, w_left, w_left_gate) * band_valid[:, None, None] * valid[None, :, None]).astype(jnp.bfloat16)
    gate = jax.nn.sigmoid(jnp.dot(normed, w_gate_out, preferred_element_type=jnp.float32)).astype(jnp.bfloat16)
    left_wide = left.astype(jnp.float32)

    def product_block(block):
        return jnp.einsum('ikc,jkc->ijc', left_wide, block.astype(jnp.float32))
    pieces = lax.map(product_block, right)
    product = jnp.transpose(pieces, (1, 0, 2, 3)).reshape(BAND, TOKENS, CH).astype(jnp.bfloat16)
    product_normed = layer_norm(product, norm_out_gain).astype(jnp.bfloat16)
    projected = jnp.dot(product_normed, w_out, preferred_element_type=jnp.float32)
    return (projected * gate.astype(jnp.float32)).astype(jnp.bfloat16)
```

```python
import functools

import jax
import jax.numpy as jnp
from jax import lax
from jax.experimental import pallas as pl
from jax.experimental.pallas import tpu as pltpu
from jax.sharding import PartitionSpec as P

BAND_DEV = 2
MESH = pl.DeviceIdType.MESH
F32 = jnp.float32
BF16 = jnp.bfloat16


def dot(a, b):
    return jnp.dot(a, b, preferred_element_type=F32)


def sigmoid(x):
    return 0.5 + 0.5 * jnp.tanh(0.5 * x)


def normalise(x, mean_w, gain):
    xc = x.astype(F32) - dot(x, mean_w)
    var = dot((xc * xc).astype(BF16), mean_w)
    return (xc * lax.rsqrt(var + 1e-05) * gain).astype(BF16)


def kernel(
    R,
    LN,
    start_ref,
    pair,
    col_valid,
    row_valid,
    left_valid,
    mean_in,
    gain_in,
    w_right2,
    w_left2,
    w_gate,
    mean_out,
    gain_out,
    w_out2,
    out,
    right,
    send_a,
    recv_a,
    send_b,
    recv_b,
    left_all,
    left_dup,
    gate,
    partial,
    p_send,
    p_recv,
    a_sem,
    b_send_sem,
    b_recv_sem,
    l_send_sem,
    f_send_sem,
    l_recv_sem,
    p_send_sem,
    p_recv_sem,
):
    rows_dev, cols, width = pair.shape
    half = rows_dev // 2
    CH = width // 2
    Z = R // 2
    me = lax.axis_index("row")
    lane = lax.axis_index("chan")
    z, core = me // 2, me % 2
    sib = me + 1 - 2 * core
    start = start_ref[0]

    def at(row, chan=None):
        if chan is None:
            return {"row": row}
        return {"row": row, "chan": chan}

    barrier = pltpu.get_barrier_semaphore()
    flat = me * LN + lane

    def greet(i, _):
        other = (flat + i) % (R * LN)
        pl.semaphore_signal(barrier, inc=1, device_id=at(other // LN, other % LN), device_id_type=MESH)
        return 0

    lax.fori_loop(1, R * LN, greet, 0)

    def candidate(t):
        return pair[jnp.clip(start + t - me * rows_dev, 0, rows_dev - 1)]

    def fill_a(i, _):
        t = (i // 2) * 4 + (1 - core) * 2 + i % 2
        send_a[i] = candidate(t)
        return 0

    lax.fori_loop(0, R, fill_a, 0)

    pl.semaphore_wait(barrier, R * LN - 1)
    copy_a = pltpu.make_async_remote_copy(
        src_ref=send_a, dst_ref=recv_a, send_sem=a_sem.at[0], recv_sem=a_sem.at[1],
        device_id=at(sib), device_id_type=MESH,
    )
    copy_a.start()

    g_in = gain_in[...]

    def right_rows(jp):
        x = jnp.concatenate([pair[jp], pair[jp + half]], axis=1)
        both = dot(normalise(x, mean_in[...], g_in), w_right2[...])
        right[jp] = sigmoid(both[:, width:]) * both[:, :width]

    def right_loop(lo, hi):
        def step(i, _):
            right_rows(lo + 2 * i)
            right_rows(lo + 2 * i + 1)
            return 0

        lax.fori_loop(0, (hi - lo) // 2, step, 0)

    right_loop(0, half // 8)
    copy_a.wait_recv()

    def fill_b(i, _):
        t = (i // 2) * 4 + core * 2 + i % 2
        theirs = ((start + t) // rows_dev == sib).astype(F32)
        mix = recv_a[i].astype(F32) * theirs + candidate(t).astype(F32) * (1.0 - theirs)
        send_b[i // 2, i % 2] = mix.astype(BF16)
        return 0

    lax.fori_loop(0, R, fill_b, 0)

    def copy_b(i):
        peer = (z + i) % Z
        return pltpu.make_async_remote_copy(
            src_ref=send_b.at[peer], dst_ref=recv_b.at[z],
            send_sem=b_send_sem.at[i], recv_sem=b_recv_sem.at[i],
            device_id=at(peer * 2 + core), device_id_type=MESH,
        )

    for i in range(1, Z):
        copy_b(i).start()
    recv_b[z] = send_b[z]
    right_loop(half // 8, half)
    for i in range(1, Z):
        copy_b(i).wait_recv()

    t = me * BAND_DEV
    rows = [recv_b[(start + t + i) // (2 * rows_dev), i] for i in range(2)]
    normed = normalise(jnp.concatenate(rows, axis=1), mean_in[...], g_in)
    both = dot(normed, w_left2[...])
    factor = sigmoid(both[:, width:]) * both[:, :width] * left_valid[...] * col_valid[...]
    left_all[me] = factor.astype(BF16)

    def copy_l(i):
        peer = ((z + i) % Z) * 2 + core
        return pltpu.make_async_remote_copy(
            src_ref=left_all.at[me], dst_ref=left_all.at[me],
            send_sem=l_send_sem.at[i], recv_sem=l_recv_sem.at[i, 0],
            device_id=at(sib if i == 0 else peer), device_id_type=MESH,
        )

    def forward(i):
        slot = ((z + Z - i) % Z) * 2 + core
        return pltpu.make_async_remote_copy(
            src_ref=left_all.at[slot], dst_ref=left_all.at[slot],
            send_sem=f_send_sem.at[i], recv_sem=l_recv_sem.at[i, 1],
            device_id=at(sib), device_id_type=MESH,
        )

    for i in range(1, Z):
        copy_l(i).start()
    copy_l(0).start()
    for i in range(2):
        gate[i] = sigmoid(dot(normed[:, i * width:(i + 1) * width], w_gate[...])).astype(BF16)

    low = lax.broadcasted_iota(jnp.int32, (cols, width), 1) < CH
    home = me // (R // LN)
    slot_out = (me % (R // LN)) * LN + lane

    def p_copy(s, send_slot):
        return pltpu.make_async_remote_copy(
            src_ref=p_send.at[s], dst_ref=p_recv.at[slot_out],
            send_sem=p_send_sem.at[s], recv_sem=p_recv_sem.at[slot_out],
            device_id=at(s, home), device_id_type=MESH,
        )

    def is_self(s):
        return jnp.logical_and(s == me, home == lane)

    def group_product(zz):
        for b in range(2):
            x = left_all[zz * 2 + b].astype(F32)
            turned = pltpu.roll(x, CH, 1)
            left_dup[2 * b] = jnp.where(low, x, turned)
            left_dup[2 * b + 1] = jnp.where(low, turned, x)

        def step(jg, _):
            def part(kc, acc):
                acc = list(acc)
                for k8 in range(8):
                    here = pl.ds(pl.multiple_of(kc * 64 + k8 * 8, 8), 8)
                    ls = [left_dup[a, here] for a in range(4)]
                    rs = [right[jg * 4 + b, here] for b in range(4)]
                    for a in range(4):
                        for b in range(4):
                            acc[4 * a + b] = acc[4 * a + b] + ls[a] * rs[b]
                return tuple(acc)

            acc = lax.fori_loop(0, cols // 64, part, (jnp.zeros((8, width), F32),) * 16)
            for a in range(4):
                for b in range(4):
                    partial[a, jg * 4 + b] = acc[4 * a + b]
            return 0

        lax.fori_loop(0, half // 4, step, 0)
        for b in range(2):
            s = zz * 2 + b
            for i in range(2):
                total = jnp.sum(partial[2 * b + i], axis=1) * row_valid[...]
                p_send[s, i] = total.astype(BF16)

            @pl.when(is_self(s))
            def _():
                p_recv[slot_out] = p_send[s]

            @pl.when(jnp.logical_not(is_self(s)))
            def _():
                p_copy(s, b).start()

    copy_l(0).wait_recv()
    group_product(z)
    for i in range(1, Z):
        copy_l(i).wait_recv()
        forward(i).start()

    def rest(i, _):
        forward(i).wait_recv()
        group_product((z + Z - i) % Z)
        return 0

    lax.fori_loop(1, Z, rest, 0)

    own_slot = jnp.where(home == lane, slot_out, R)
    for src in range(R // LN):
        total = None
        for other in range(LN):
            q = src * LN + other

            @pl.when(q != own_slot)
            def _():
                pltpu.make_async_remote_copy(
                    src_ref=p_send.at[0], dst_ref=p_recv.at[q],
                    send_sem=p_send_sem.at[0], recv_sem=p_recv_sem.at[q],
                    device_id=at(sib), device_id_type=MESH,
                ).wait_recv()

            piece = p_recv[q].astype(F32)
            total = piece if total is None else total + piece
        product = total.astype(BF16).reshape(2 * half, width)
        normed_p = normalise(product, mean_out[...], gain_out[...])
        projected = dot(normed_p, w_out2[...])
        for i in range(2):
            for h in range(2):
                here = slice(src * rows_dev + h * half, src * rows_dev + (h + 1) * half)
                opener = gate[i, here].astype(F32)
                mine = projected[i * half:(i + 1) * half, h * width:(h + 1) * width]
                out[i, here] = (mine * opener).astype(BF16)

    copy_a.wait_send()
    for i in range(1, Z):
        copy_b(i).wait_send()
        copy_l(i).wait_send()
        forward(i).wait_send()
    copy_l(0).wait_send()

    def drain(s, _):
        @pl.when(jnp.logical_not(is_self(s)))
        def _():
            p_copy(s, 0).wait_send()

        return 0

    lax.fori_loop(0, R, drain, 0)


def twice(a):
    zero = jnp.zeros_like(a)
    return jnp.concatenate([jnp.concatenate([a, zero], 1), jnp.concatenate([zero, a], 1)], 0)


def body(
    R,
    LN,
    pair,
    token_mask,
    band_start,
    w_left,
    w_left_gate,
    w_right,
    w_right_gate,
    w_gate_out,
    w_out,
    norm_in_gain,
    norm_out_gain,
):
    rows_dev, cols, width = pair.shape
    half = rows_dev // 2
    CH = width // 2
    place = lax.axis_index("row")
    lane = lax.axis_index("chan")
    valid = token_mask.astype(F32)
    row_valid = lax.dynamic_slice_in_dim(valid, place * rows_dev, rows_dev)
    col_valid = lax.dynamic_slice_in_dim(valid, lane * cols, cols)
    left_valid = lax.dynamic_slice_in_dim(valid, band_start[0] + place * BAND_DEV, BAND_DEV)
    col_valid = jnp.broadcast_to(col_valid[:, None], (cols, width))
    row_valid = jnp.repeat(row_valid.reshape(2, half).T, CH, axis=1)
    left_valid = jnp.repeat(left_valid, CH)[None, :]
    mean_in = twice(jnp.full((width, width), 1 / width, BF16))
    mean_out = twice(jnp.full((CH, CH), 1 / CH, BF16))
    gain_in = jnp.tile(norm_in_gain, 2)[None, :]
    gain_out = jnp.tile(norm_out_gain, 2)[None, :]
    w_right2 = jnp.concatenate([twice(w_right), twice(w_right_gate)], 1)
    w_left2 = jnp.concatenate([twice(w_left), twice(w_left_gate)], 1)
    Z = R // 2
    dma = pltpu.SemaphoreType.DMA
    vmem = pl.BlockSpec(memory_space=pltpu.VMEM)
    return pl.pallas_call(
        functools.partial(kernel, R, LN),
        out_shape=jax.ShapeDtypeStruct((BAND_DEV, cols, width), BF16),
        in_specs=[pl.BlockSpec(memory_space=pltpu.SMEM)] + [vmem] * 12,
        out_specs=vmem,
        scratch_shapes=[
            pltpu.VMEM((half, cols, width), F32),
            pltpu.VMEM((R, cols, width), BF16),
            pltpu.VMEM((R, cols, width), BF16),
            pltpu.VMEM((Z, 2, cols, width), BF16),
            pltpu.VMEM((Z, 2, cols, width), BF16),
            pltpu.VMEM((R, cols, width), BF16),
            pltpu.VMEM((4, cols, width), F32),
            pltpu.VMEM((2, cols, width), BF16),
            pltpu.VMEM((4, half, 8, width), F32),
            pltpu.VMEM((R, 2, half, width), BF16),
            pltpu.VMEM((R, 2, half, width), BF16),
            dma((2,)),
            dma((Z,)),
            dma((Z,)),
            dma((Z,)),
            dma((Z,)),
            dma((Z, 2)),
            dma((R,)),
            dma((R,)),
        ],
        compiler_params=pltpu.CompilerParams(
            collective_id=0, has_side_effects=True, vmem_limit_bytes=56 * 2**20
        ),
    )(
        band_start, pair, col_valid, row_valid, left_valid, mean_in, gain_in,
        w_right2, w_left2, w_gate_out, mean_out, gain_out, twice(w_out),
    )


def solution(mesh):
    R, LN = mesh.shape["row"], mesh.shape["chan"]
    return jax.shard_map(
        functools.partial(body, R, LN),
        mesh=mesh,
        in_specs=(
            P(("group", "row"), "chan", None),
            P("group"),
            P("group"),
            P(),
            P(),
            P(),
            P(),
            P(),
            P(),
            P(),
            P(),
        ),
        out_specs=P(("group", "row"), "chan", None),
        check_vma=False,
    )
```

```python
import functools

import jax
import jax.numpy as jnp
from jax import lax
from jax.experimental import pallas as pl
from jax.experimental.pallas import tpu as pltpu
from jax.sharding import PartitionSpec as P

BAND_DEV = 2
MESH = pl.DeviceIdType.MESH
F32 = jnp.float32
BF16 = jnp.bfloat16


def dot(a, b):
    return jnp.dot(a, b, preferred_element_type=F32)


def sigmoid(x):
    return 0.5 + 0.5 * jnp.tanh(0.5 * x)


def normalise(x, mean_w, gain):
    xc = x.astype(F32) - dot(x, mean_w)
    var = dot((xc * xc).astype(BF16), mean_w)
    return (xc * lax.rsqrt(var + 1e-05) * gain).astype(BF16)


def kernel(
    R,
    LN,
    start_ref,
    mask_ref,
    pair_hbm,
    w_left_t,
    w_left_gate_t,
    w_right_t,
    w_right_gate_t,
    w_gate,
    w_out,
    gain_in_ref,
    gain_out_ref,
    out,
    right,
    send_a,
    recv_a,
    send_b,
    recv_b,
    left_all,
    left_dup,
    gate,
    partial,
    p_send,
    p_recv,
    pair,
    col_valid,
    row_valid,
    mean_in,
    mean_out,
    w_right2,
    w_left2,
    pair_sem,
    a_sem,
    b_send_sem,
    b_recv_sem,
    l_send_sem,
    f_send_sem,
    l_recv_sem,
    p_send_sem,
    p_recv_sem,
):
    rows_dev, cols, width = pair.shape
    half = rows_dev // 2
    CH = width // 2
    Z = R // 2
    me = lax.axis_index("row")
    lane = lax.axis_index("chan")
    z, core = me // 2, me % 2
    sib = me + 1 - 2 * core
    start = start_ref[0]

    def at(row, chan=None):
        if chan is None:
            return {"row": row}
        return {"row": row, "chan": chan}

    load = pltpu.make_async_copy(pair_hbm, pair, pair_sem)
    load.start()

    barrier = pltpu.get_barrier_semaphore()
    flat = me * LN + lane

    def greet(i, _):
        other = (flat + i) % (R * LN)
        pl.semaphore_signal(barrier, inc=1, device_id=at(other // LN, other % LN), device_id_type=MESH)
        return 0

    lax.fori_loop(1, R * LN, greet, 0)

    def same_block(size, block):
        i = lax.broadcasted_iota(jnp.int32, (size, size), 0) // block
        j = lax.broadcasted_iota(jnp.int32, (size, size), 1) // block
        return jnp.where(i == j, 1.0 / block, 0.0).astype(BF16)

    def pair_weights(value_t, gate_t):
        zero = jnp.zeros((CH, width), BF16)
        parts = [(value_t, zero), (zero, value_t), (gate_t, zero), (zero, gate_t)]
        return jnp.concatenate([jnp.concatenate(p, 1) for p in parts], 0).T

    mean_in[...] = same_block(2 * width, width)
    mean_out[...] = same_block(width, CH)
    w_right2[...] = pair_weights(w_right_t[...], w_right_gate_t[...])
    w_left2[...] = pair_weights(w_left_t[...], w_left_gate_t[...])
    tokens = mask_ref.shape[1]
    valid = mask_ref[...].astype(F32)
    ones = jnp.ones((tokens, width), BF16)

    def picked(count, first):
        token = lax.broadcasted_iota(jnp.int32, (count, tokens), 1)
        wanted = lax.broadcasted_iota(jnp.int32, (count, tokens), 0) + first
        return dot(jnp.where(token == wanted, valid, 0.0).astype(BF16), ones)

    col_valid[...] = picked(cols, lane * cols)
    left_half = lax.broadcasted_iota(jnp.int32, (half, width), 1) < CH
    row_valid[...] = jnp.where(
        left_half, picked(half, me * rows_dev), picked(half, me * rows_dev + half)
    )
    band_token = lax.broadcasted_iota(jnp.int32, (1, tokens), 1) - start - me * BAND_DEV
    band_valid = [
        jnp.sum(jnp.where(band_token == i, valid, 0.0), axis=1, keepdims=True) for i in range(2)
    ]
    left_valid = jnp.where(
        lax.broadcasted_iota(jnp.int32, (1, width), 1) < CH, band_valid[0], band_valid[1]
    )
    g_in = jnp.concatenate([gain_in_ref[...]] * 2, axis=1)
    g_out = jnp.concatenate([gain_out_ref[...]] * 2, axis=1)
    zero_out = jnp.zeros((CH, width), BF16)
    w_out2 = jnp.concatenate(
        [jnp.concatenate([w_out[...], zero_out], 1), jnp.concatenate([zero_out, w_out[...]], 1)], 0
    )
    load.wait()

    def candidate(t):
        return pair[jnp.clip(start + t - me * rows_dev, 0, rows_dev - 1)]

    def fill_a(i, _):
        t = (i // 2) * 4 + (1 - core) * 2 + i % 2
        send_a[i] = candidate(t)
        return 0

    lax.fori_loop(0, R, fill_a, 0)

    pl.semaphore_wait(barrier, R * LN - 1)
    copy_a = pltpu.make_async_remote_copy(
        src_ref=send_a, dst_ref=recv_a, send_sem=a_sem.at[0], recv_sem=a_sem.at[1],
        device_id=at(sib), device_id_type=MESH,
    )
    copy_a.start()

    def right_rows(jp):
        x = jnp.concatenate([pair[jp], pair[jp + half]], axis=1)
        both = dot(normalise(x, mean_in[...], g_in), w_right2[...])
        right[jp] = sigmoid(both[:, width:]) * both[:, :width]

    def right_loop(lo, hi):
        def step(i, _):
            right_rows(lo + 2 * i)
            right_rows(lo + 2 * i + 1)
            return 0

        lax.fori_loop(0, (hi - lo) // 2, step, 0)

    right_loop(0, half // 8)
    copy_a.wait_recv()

    def fill_b(i, _):
        t = (i // 2) * 4 + core * 2 + i % 2
        theirs = ((start + t) // rows_dev == sib).astype(F32)
        mix = recv_a[i].astype(F32) * theirs + candidate(t).astype(F32) * (1.0 - theirs)
        send_b[i // 2, i % 2] = mix.astype(BF16)
        return 0

    lax.fori_loop(0, R, fill_b, 0)

    def copy_b(i):
        peer = (z + i) % Z
        return pltpu.make_async_remote_copy(
            src_ref=send_b.at[peer], dst_ref=recv_b.at[z],
            send_sem=b_send_sem.at[i], recv_sem=b_recv_sem.at[i],
            device_id=at(peer * 2 + core), device_id_type=MESH,
        )

    for i in range(1, Z):
        copy_b(i).start()
    recv_b[z] = send_b[z]
    right_loop(half // 8, half)
    for i in range(1, Z):
        copy_b(i).wait_recv()

    t = me * BAND_DEV
    rows = [recv_b[(start + t + i) // (2 * rows_dev), i] for i in range(2)]
    normed = normalise(jnp.concatenate(rows, axis=1), mean_in[...], g_in)
    both = dot(normed, w_left2[...])
    factor = sigmoid(both[:, width:]) * both[:, :width] * left_valid * col_valid[...]
    left_all[me] = factor.astype(BF16)

    def copy_l(i):
        peer = ((z + i) % Z) * 2 + core
        return pltpu.make_async_remote_copy(
            src_ref=left_all.at[me], dst_ref=left_all.at[me],
            send_sem=l_send_sem.at[i], recv_sem=l_recv_sem.at[i, 0],
            device_id=at(sib if i == 0 else peer), device_id_type=MESH,
        )

    def forward(i):
        slot = ((z + Z - i) % Z) * 2 + core
        return pltpu.make_async_remote_copy(
            src_ref=left_all.at[slot], dst_ref=left_all.at[slot],
            send_sem=f_send_sem.at[i], recv_sem=l_recv_sem.at[i, 1],
            device_id=at(sib), device_id_type=MESH,
        )

    for i in range(1, Z):
        copy_l(i).start()
    copy_l(0).start()
    for i in range(2):
        gate[i] = sigmoid(dot(normed[:, i * width:(i + 1) * width], w_gate[...])).astype(BF16)

    low = lax.broadcasted_iota(jnp.int32, (cols, width), 1) < CH
    home = me // (R // LN)
    slot_out = (me % (R // LN)) * LN + lane

    def p_copy(s, send_slot):
        return pltpu.make_async_remote_copy(
            src_ref=p_send.at[s], dst_ref=p_recv.at[slot_out],
            send_sem=p_send_sem.at[s], recv_sem=p_recv_sem.at[slot_out],
            device_id=at(s, home), device_id_type=MESH,
        )

    def is_self(s):
        return jnp.logical_and(s == me, home == lane)

    def group_product(zz):
        for b in range(2):
            x = left_all[zz * 2 + b].astype(F32)
            turned = pltpu.roll(x, CH, 1)
            left_dup[2 * b] = jnp.where(low, x, turned)
            left_dup[2 * b + 1] = jnp.where(low, turned, x)

        def step(jg, _):
            def part(kc, acc):
                acc = list(acc)
                for k8 in range(8):
                    here = pl.ds(pl.multiple_of(kc * 64 + k8 * 8, 8), 8)
                    ls = [left_dup[a, here] for a in range(4)]
                    rs = [right[jg * 4 + b, here] for b in range(4)]
                    for a in range(4):
                        for b in range(4):
                            acc[4 * a + b] = acc[4 * a + b] + ls[a] * rs[b]
                return tuple(acc)

            acc = lax.fori_loop(0, cols // 64, part, (jnp.zeros((8, width), F32),) * 16)
            for a in range(4):
                for b in range(4):
                    partial[a, jg * 4 + b] = acc[4 * a + b]
            return 0

        lax.fori_loop(0, half // 4, step, 0)
        for b in range(2):
            s = zz * 2 + b
            for i in range(2):
                total = jnp.sum(partial[2 * b + i], axis=1) * row_valid[...]
                p_send[s, i] = total.astype(BF16)

            @pl.when(is_self(s))
            def _():
                p_recv[slot_out] = p_send[s]

            @pl.when(jnp.logical_not(is_self(s)))
            def _():
                p_copy(s, b).start()

    copy_l(0).wait_recv()
    group_product(z)
    for i in range(1, Z):
        copy_l(i).wait_recv()
        forward(i).start()

    def rest(i, _):
        forward(i).wait_recv()
        group_product((z + Z - i) % Z)
        return 0

    lax.fori_loop(1, Z, rest, 0)

    own_slot = jnp.where(home == lane, slot_out, R)
    for src in range(R // LN):
        total = None
        for other in range(LN):
            q = src * LN + other

            @pl.when(q != own_slot)
            def _():
                pltpu.make_async_remote_copy(
                    src_ref=p_send.at[0], dst_ref=p_recv.at[q],
                    send_sem=p_send_sem.at[0], recv_sem=p_recv_sem.at[q],
                    device_id=at(sib), device_id_type=MESH,
                ).wait_recv()

            piece = p_recv[q].astype(F32)
            total = piece if total is None else total + piece
        product = total.astype(BF16).reshape(2 * half, width)
        normed_p = normalise(product, mean_out[...], g_out)
        projected = dot(normed_p, w_out2)
        for i in range(2):
            for h in range(2):
                here = slice(src * rows_dev + h * half, src * rows_dev + (h + 1) * half)
                opener = gate[i, here].astype(F32)
                mine = projected[i * half:(i + 1) * half, h * width:(h + 1) * width]
                out[i, here] = (mine * opener).astype(BF16)

    copy_a.wait_send()
    for i in range(1, Z):
        copy_b(i).wait_send()
        copy_l(i).wait_send()
        forward(i).wait_send()
    copy_l(0).wait_send()

    def drain(s, _):
        @pl.when(jnp.logical_not(is_self(s)))
        def _():
            p_copy(s, 0).wait_send()

        return 0

    lax.fori_loop(0, R, drain, 0)


def body(
    R,
    LN,
    pair,
    token_mask,
    band_start,
    w_left,
    w_left_gate,
    w_right,
    w_right_gate,
    w_gate_out,
    w_out,
    norm_in_gain,
    norm_out_gain,
):
    rows_dev, cols, width = pair.shape
    half = rows_dev // 2
    CH = width // 2
    Z = R // 2
    dma = pltpu.SemaphoreType.DMA
    vmem = pl.BlockSpec(memory_space=pltpu.VMEM)
    return pl.pallas_call(
        functools.partial(kernel, R, LN),
        out_shape=jax.ShapeDtypeStruct((BAND_DEV, cols, width), BF16),
        in_specs=[pl.BlockSpec(memory_space=pltpu.SMEM), vmem, pl.BlockSpec(memory_space=pl.ANY)] + [vmem] * 8,
        out_specs=vmem,
        scratch_shapes=[
            pltpu.VMEM((half, cols, width), F32),
            pltpu.VMEM((R, cols, width), BF16),
            pltpu.VMEM((R, cols, width), BF16),
            pltpu.VMEM((Z, 2, cols, width), BF16),
            pltpu.VMEM((Z, 2, cols, width), BF16),
            pltpu.VMEM((R, cols, width), BF16),
            pltpu.VMEM((4, cols, width), F32),
            pltpu.VMEM((2, cols, width), BF16),
            pltpu.VMEM((4, half, 8, width), F32),
            pltpu.VMEM((R, 2, half, width), BF16),
            pltpu.VMEM((R, 2, half, width), BF16),
            pltpu.VMEM((rows_dev, cols, width), BF16),
            pltpu.VMEM((cols, width), F32),
            pltpu.VMEM((half, width), F32),
            pltpu.VMEM((2 * width, 2 * width), BF16),
            pltpu.VMEM((width, width), BF16),
            pltpu.VMEM((2 * width, 2 * width), BF16),
            pltpu.VMEM((2 * width, 2 * width), BF16),
            dma,
            dma((2,)),
            dma((Z,)),
            dma((Z,)),
            dma((Z,)),
            dma((Z,)),
            dma((Z, 2)),
            dma((R,)),
            dma((R,)),
        ],
        compiler_params=pltpu.CompilerParams(
            collective_id=0, has_side_effects=True, vmem_limit_bytes=56 * 2**20
        ),
    )(
        band_start, token_mask[None], pair, w_left.T, w_left_gate.T, w_right.T, w_right_gate.T,
        w_gate_out, w_out, norm_in_gain[None], norm_out_gain[None],
    )


def solution(mesh):
    R, LN = mesh.shape["row"], mesh.shape["chan"]
    return jax.shard_map(
        functools.partial(body, R, LN),
        mesh=mesh,
        in_specs=(
            P(("group", "row"), "chan", None),
            P("group"),
            P("group"),
            P(),
            P(),
            P(),
            P(),
            P(),
            P(),
            P(),
            P(),
        ),
        out_specs=P(("group", "row"), "chan", None),
        check_vma=False,
    )
```

```python
import functools

import jax
import jax.numpy as jnp
from jax import lax
from jax.experimental import pallas as pl
from jax.experimental.pallas import tpu as pltpu
from jax.sharding import PartitionSpec as P

BAND_DEV = 2
MESH = pl.DeviceIdType.MESH
F32 = jnp.float32
BF16 = jnp.bfloat16


def dot(a, b):
    return jnp.dot(a, b, preferred_element_type=F32)


def sigmoid(x):
    return 0.5 + 0.5 * jnp.tanh(0.5 * x)


def normalise(x, mean_w, gain):
    xc = x.astype(F32) - dot(x, mean_w)
    var = dot((xc * xc).astype(BF16), mean_w)
    return (xc * lax.rsqrt(var + 1e-05) * gain).astype(BF16)


def kernel(
    R,
    LN,
    start_ref,
    mask_ref,
    pair_hbm,
    w_left_t,
    w_left_gate_t,
    w_right_t,
    w_right_gate_t,
    w_gate,
    w_out,
    gain_in_ref,
    gain_out_ref,
    out,
    right,
    send_a,
    recv_a,
    send_b,
    recv_b,
    left_all,
    left_dup,
    gate,
    partial,
    p_send,
    p_recv,
    pair,
    col_valid,
    row_valid,
    mean_in,
    mean_out,
    w_right2,
    w_left2,
    pair_sem,
    a_sem,
    b_send_sem,
    b_recv_sem,
    l_send_sem,
    f_send_sem,
    l_recv_sem,
    p_send_sem,
    p_recv_sem,
):
    rows_dev, cols, width = pair.shape
    half = rows_dev // 2
    CH = width // 2
    Z = R // 2
    me = lax.axis_index("row")
    lane = lax.axis_index("chan")
    z, core = me // 2, me % 2
    sib = me + 1 - 2 * core
    start = start_ref[0]

    def at(row, chan=None):
        if chan is None:
            return {"row": row}
        return {"row": row, "chan": chan}

    load = pltpu.make_async_copy(pair_hbm, pair, pair_sem)
    load.start()

    barrier = pltpu.get_barrier_semaphore()
    flat = me * LN + lane

    def greet(i, _):
        other = (flat + i) % (R * LN)
        pl.semaphore_signal(barrier, inc=1, device_id=at(other // LN, other % LN), device_id_type=MESH)
        return 0

    lax.fori_loop(1, R * LN, greet, 0)

    load.wait()

    def candidate(t):
        return pair[jnp.clip(start + t - me * rows_dev, 0, rows_dev - 1)]

    def fill_a(i, _):
        t = (i // 2) * 4 + (1 - core) * 2 + i % 2
        send_a[i] = candidate(t)
        return 0

    lax.fori_loop(0, R, fill_a, 0)

    pl.semaphore_wait(barrier, R * LN - 1)
    copy_a = pltpu.make_async_remote_copy(
        src_ref=send_a, dst_ref=recv_a, send_sem=a_sem.at[0], recv_sem=a_sem.at[1],
        device_id=at(sib), device_id_type=MESH,
    )
    copy_a.start()

    def same_block(size, block):
        i = lax.broadcasted_iota(jnp.int32, (size, size), 0) // block
        j = lax.broadcasted_iota(jnp.int32, (size, size), 1) // block
        return jnp.where(i == j, 1.0 / block, 0.0).astype(BF16)

    def pair_weights(value_t, gate_t):
        zero = jnp.zeros((CH, width), BF16)
        parts = [(value_t, zero), (zero, value_t), (gate_t, zero), (zero, gate_t)]
        return jnp.concatenate([jnp.concatenate(p, 1) for p in parts], 0).T

    mean_in[...] = same_block(2 * width, width)
    mean_out[...] = same_block(width, CH)
    w_right2[...] = pair_weights(w_right_t[...], w_right_gate_t[...])
    w_left2[...] = pair_weights(w_left_t[...], w_left_gate_t[...])
    tokens = mask_ref.shape[1]
    valid = mask_ref[...].astype(F32)
    ones = jnp.ones((tokens, width), BF16)

    def picked(count, first):
        token = lax.broadcasted_iota(jnp.int32, (count, tokens), 1)
        wanted = lax.broadcasted_iota(jnp.int32, (count, tokens), 0) + first
        return dot(jnp.where(token == wanted, valid, 0.0).astype(BF16), ones)

    col_valid[...] = picked(cols, lane * cols)
    left_half = lax.broadcasted_iota(jnp.int32, (half, width), 1) < CH
    row_valid[...] = jnp.where(
        left_half, picked(half, me * rows_dev), picked(half, me * rows_dev + half)
    )
    band_token = lax.broadcasted_iota(jnp.int32, (1, tokens), 1) - start - me * BAND_DEV
    band_valid = [
        jnp.sum(jnp.where(band_token == i, valid, 0.0), axis=1, keepdims=True) for i in range(2)
    ]
    left_valid = jnp.where(
        lax.broadcasted_iota(jnp.int32, (1, width), 1) < CH, band_valid[0], band_valid[1]
    )
    g_in = jnp.concatenate([gain_in_ref[...]] * 2, axis=1)
    g_out = jnp.concatenate([gain_out_ref[...]] * 2, axis=1)
    zero_out = jnp.zeros((CH, width), BF16)
    w_out2 = jnp.concatenate(
        [jnp.concatenate([w_out[...], zero_out], 1), jnp.concatenate([zero_out, w_out[...]], 1)], 0
    )

    def right_rows(jp):
        x = jnp.concatenate([pair[jp], pair[jp + half]], axis=1)
        both = dot(normalise(x, mean_in[...], g_in), w_right2[...])
        right[jp] = sigmoid(both[:, width:]) * both[:, :width]

    def right_loop(lo, hi):
        def step(i, _):
            right_rows(lo + 2 * i)
            right_rows(lo + 2 * i + 1)
            return 0

        lax.fori_loop(0, (hi - lo) // 2, step, 0)

    right_loop(0, half // 8)
    copy_a.wait_recv()

    def fill_b(i, _):
        t = (i // 2) * 4 + core * 2 + i % 2
        theirs = ((start + t) // rows_dev == sib).astype(F32)
        mix = recv_a[i].astype(F32) * theirs + candidate(t).astype(F32) * (1.0 - theirs)
        send_b[i // 2, i % 2] = mix.astype(BF16)
        return 0

    lax.fori_loop(0, R, fill_b, 0)

    def copy_b(i):
        peer = (z + i) % Z
        return pltpu.make_async_remote_copy(
            src_ref=send_b.at[peer], dst_ref=recv_b.at[z],
            send_sem=b_send_sem.at[i], recv_sem=b_recv_sem.at[i],
            device_id=at(peer * 2 + core), device_id_type=MESH,
        )

    for i in sorted(range(1, Z), key=lambda i: -abs(i - Z // 2)):
        copy_b(i).start()
    recv_b[z] = send_b[z]
    right_loop(half // 8, half)
    for i in range(1, Z):
        copy_b(i).wait_recv()

    t = me * BAND_DEV
    rows = [recv_b[(start + t + i) // (2 * rows_dev), i] for i in range(2)]
    normed = normalise(jnp.concatenate(rows, axis=1), mean_in[...], g_in)
    both = dot(normed, w_left2[...])
    factor = sigmoid(both[:, width:]) * both[:, :width] * left_valid * col_valid[...]
    left_all[me] = factor.astype(BF16)

    def copy_l(i, peer=None):
        if peer is None:
            peer = sib if i == 0 else ((z + i) % Z) * 2 + core
        return pltpu.make_async_remote_copy(
            src_ref=left_all.at[me], dst_ref=left_all.at[me],
            send_sem=l_send_sem.at[i], recv_sem=l_recv_sem.at[i, 0],
            device_id=at(peer), device_id_type=MESH,
        )

    def forward(i):
        slot = ((z + Z - i) % Z) * 2 + core
        return pltpu.make_async_remote_copy(
            src_ref=left_all.at[slot], dst_ref=left_all.at[slot],
            send_sem=f_send_sem.at[i], recv_sem=l_recv_sem.at[i, 1],
            device_id=at(sib), device_id_type=MESH,
        )

    for i in sorted(range(1, Z), key=lambda i: -abs(i - Z // 2)):
        copy_l(i).start()
    copy_l(0).start()
    for i in range(2):
        gate[i] = sigmoid(dot(normed[:, i * width:(i + 1) * width], w_gate[...])).astype(BF16)

    low = lax.broadcasted_iota(jnp.int32, (cols, width), 1) < CH
    home = me // (R // LN)
    slot_out = (me % (R // LN)) * LN + lane

    def p_copy(s, send_slot):
        return pltpu.make_async_remote_copy(
            src_ref=p_send.at[s], dst_ref=p_recv.at[slot_out],
            send_sem=p_send_sem.at[s], recv_sem=p_recv_sem.at[slot_out],
            device_id=at(s, home), device_id_type=MESH,
        )

    def is_self(s):
        return jnp.logical_and(s == me, home == lane)

    def group_product(zz):
        for b in range(2):
            x = left_all[zz * 2 + b].astype(F32)
            turned = pltpu.roll(x, CH, 1)
            left_dup[2 * b] = jnp.where(low, x, turned)
            left_dup[2 * b + 1] = jnp.where(low, turned, x)

        def step(jg, _):
            def part(kc, acc):
                acc = list(acc)
                for k8 in range(8):
                    here = pl.ds(pl.multiple_of(kc * 64 + k8 * 8, 8), 8)
                    ls = [left_dup[a, here] for a in range(4)]
                    rs = [right[jg * 4 + b, here] for b in range(4)]
                    for a in range(4):
                        for b in range(4):
                            acc[4 * a + b] = acc[4 * a + b] + ls[a] * rs[b]
                return tuple(acc)

            acc = lax.fori_loop(0, cols // 64, part, (jnp.zeros((8, width), F32),) * 16)
            for a in range(4):
                for b in range(4):
                    partial[a, jg * 4 + b] = acc[4 * a + b]
            return 0

        lax.fori_loop(0, half // 4, step, 0)
        for b in range(2):
            s = zz * 2 + b
            for i in range(2):
                total = jnp.sum(partial[2 * b + i], axis=1) * row_valid[...]
                p_send[s, i] = total.astype(BF16)

            @pl.when(is_self(s))
            def _():
                p_recv[slot_out] = p_send[s]

            @pl.when(jnp.logical_not(is_self(s)))
            def _():
                p_copy(s, b).start()

    copy_l(0).wait_recv()
    group_product(z)
    copy_l(1).wait_recv()
    forward(1).start()

    def rest(i, _):
        @pl.when(i < Z - 1)
        def _():
            copy_l(i + 1, sib).wait_recv()
            forward(i + 1).start()

        forward(i).wait_recv()
        group_product((z + Z - i) % Z)
        return 0

    lax.fori_loop(1, Z, rest, 0)

    own_slot = jnp.where(home == lane, slot_out, R)
    for src in range(R // LN):
        total = None
        for other in range(LN):
            q = src * LN + other

            @pl.when(q != own_slot)
            def _():
                pltpu.make_async_remote_copy(
                    src_ref=p_send.at[0], dst_ref=p_recv.at[q],
                    send_sem=p_send_sem.at[0], recv_sem=p_recv_sem.at[q],
                    device_id=at(sib), device_id_type=MESH,
                ).wait_recv()

            piece = p_recv[q].astype(F32)
            total = piece if total is None else total + piece
        product = total.astype(BF16).reshape(2 * half, width)
        normed_p = normalise(product, mean_out[...], g_out)
        projected = dot(normed_p, w_out2)
        for i in range(2):
            for h in range(2):
                here = slice(src * rows_dev + h * half, src * rows_dev + (h + 1) * half)
                opener = gate[i, here].astype(F32)
                mine = projected[i * half:(i + 1) * half, h * width:(h + 1) * width]
                out[i, here] = (mine * opener).astype(BF16)

    copy_a.wait_send()
    for i in range(1, Z):
        copy_b(i).wait_send()
        copy_l(i).wait_send()
        forward(i).wait_send()
    copy_l(0).wait_send()

    def drain(s, _):
        @pl.when(jnp.logical_not(is_self(s)))
        def _():
            p_copy(s, 0).wait_send()

        return 0

    lax.fori_loop(0, R, drain, 0)


def body(
    R,
    LN,
    pair,
    token_mask,
    band_start,
    w_left,
    w_left_gate,
    w_right,
    w_right_gate,
    w_gate_out,
    w_out,
    norm_in_gain,
    norm_out_gain,
):
    rows_dev, cols, width = pair.shape
    half = rows_dev // 2
    CH = width // 2
    Z = R // 2
    dma = pltpu.SemaphoreType.DMA
    vmem = pl.BlockSpec(memory_space=pltpu.VMEM)
    return pl.pallas_call(
        functools.partial(kernel, R, LN),
        out_shape=jax.ShapeDtypeStruct((BAND_DEV, cols, width), BF16),
        in_specs=[pl.BlockSpec(memory_space=pltpu.SMEM), vmem, pl.BlockSpec(memory_space=pl.ANY)] + [vmem] * 8,
        out_specs=vmem,
        scratch_shapes=[
            pltpu.VMEM((half, cols, width), F32),
            pltpu.VMEM((R, cols, width), BF16),
            pltpu.VMEM((R, cols, width), BF16),
            pltpu.VMEM((Z, 2, cols, width), BF16),
            pltpu.VMEM((Z, 2, cols, width), BF16),
            pltpu.VMEM((R, cols, width), BF16),
            pltpu.VMEM((4, cols, width), F32),
            pltpu.VMEM((2, cols, width), BF16),
            pltpu.VMEM((4, half, 8, width), F32),
            pltpu.VMEM((R, 2, half, width), BF16),
            pltpu.VMEM((R, 2, half, width), BF16),
            pltpu.VMEM((rows_dev, cols, width), BF16),
            pltpu.VMEM((cols, width), F32),
            pltpu.VMEM((half, width), F32),
            pltpu.VMEM((2 * width, 2 * width), BF16),
            pltpu.VMEM((width, width), BF16),
            pltpu.VMEM((2 * width, 2 * width), BF16),
            pltpu.VMEM((2 * width, 2 * width), BF16),
            dma,
            dma((2,)),
            dma((Z,)),
            dma((Z,)),
            dma((Z,)),
            dma((Z,)),
            dma((Z, 2)),
            dma((R,)),
            dma((R,)),
        ],
        compiler_params=pltpu.CompilerParams(
            collective_id=0, has_side_effects=True, vmem_limit_bytes=56 * 2**20
        ),
    )(
        band_start, token_mask[None], pair, w_left.T, w_left_gate.T, w_right.T, w_right_gate.T,
        w_gate_out, w_out, norm_in_gain[None], norm_out_gain[None],
    )


def solution(mesh):
    R, LN = mesh.shape["row"], mesh.shape["chan"]
    return jax.shard_map(
        functools.partial(body, R, LN),
        mesh=mesh,
        in_specs=(
            P(("group", "row"), "chan", None),
            P("group"),
            P("group"),
            P(),
            P(),
            P(),
            P(),
            P(),
            P(),
            P(),
            P(),
        ),
        out_specs=P(("group", "row"), "chan", None),
        check_vma=False,
    )
```
